32 devices in a mesh: dp: 8 (over y, x, core), expert: 4 (over z).
Axes of the slice: x: 2, y: 2, z: 4, core: 2. Of those that a mesh axis runs over, the one named last changes fastest.
Arguments:
- tokens: bfloat16 [4096, 2048], P(('dp', 'expert')), may hold values from -6 to 6
- routes: int32 [4096, 1], P(('dp', 'expert')), may hold values from 0 to 3; in each aligned block of 128 rows (0 to 127, 128 to 255, ...) at most 40 rows name the same one
- route_gates: float32 [4096, 1], P(('dp', 'expert')), may hold values from 0.1 to 1
- w_gate: bfloat16 [4, 2048, 384], P('expert'), may hold values from -0.125 to 0.125
- w_up: bfloat16 [4, 2048, 384], P('expert'), may hold values from -0.125 to 0.125
- w_down: bfloat16 [4, 384, 2048], P('expert'), may hold values from -0.3125 to 0.3125
- cotangent: bfloat16 [4096, 2048], P(('dp', 'expert')), may hold values from -6 to 6
Outputs:
- mixed: bfloat16 [4096, 2048], P(('dp', 'expert'))
- d_tokens: bfloat16 [4096, 2048], P(('dp', 'expert'))
- d_gates: float32 [4096, 1], P(('dp', 'expert'))
- d_w_down: bfloat16 [4, 384, 2048], P('expert', 'dp')
The draws below stay inside these ranges and needn't reach their ends.
Inputs may be any that keep to these rules, and one draw needn't show every extreme that they name: `routes`: each token names exactly one expert. Among the rows of one device no expert is named more than 40 times, a bound that some block reaches in some devices' rows; every expert is named somewhere.
All inputs are finite; a program needn't handle non-finite values.
Results may differ from the reference program's by a relative error of at most 0.0058.
Values may be sent and summed in bfloat16 or wider, within the bound.
A program may use at most 64 MiB of HBM per device.

```python
import math
import jax
import jax.numpy as jnp
import numpy as np
from jax import lax

D = 2048
FF = 384
TOK_DEV = 128
TOP = 1
EXPERTS = 4
CAP = 40
TOKENS = 4096
N_DP = 8
N_EXPERT = 4


def level_of(stream_key, extent, split, least, high):
    factor_of, own = 1.0, jax.random.fold_in(stream_key, 6)
    for position, blocks in split:
        heights = jnp.exp(jax.random.uniform(jax.random.fold_in(own, position), (blocks,), jnp.float32, least / len(split), high / len(split)))
        factor_of = factor_of * jnp.repeat(heights, extent[position] // blocks).reshape([-1 if axis == position else 1 for axis in range(len(extent))])
    return factor_of


def routed_block(stream_key, own, number, rows, number_of, top, reach, skew):
    ranking = jax.random.permutation(stream_key, number_of)
    crowded, ordinary = load_shares(number_of, rows * top, reach, skew, True), load_shares(number_of, rows * top, reach, skew, False)
    places = jnp.arange(number_of)

    def named(tallies, turn):
        used = int((tallies > 0).sum())
        fixed = max(1, used // 4)
        moved = fixed + (places - fixed + turn * (used - fixed)) % max(1, number_of - fixed)
        return jnp.zeros((number_of,), jnp.int32).at[ranking[jnp.where(places < fixed, places, moved)]].set(jnp.asarray(tallies, jnp.int32))

    tallies = jnp.where(number % 4 == 0, named(crowded, number // 4), named(ordinary, number - number // 4 - 1))
    mixed = jax.random.permutation(jax.random.fold_in(own, 3), number_of)
    giver, taker = mixed[0:number_of // 2 * 2:2], mixed[1:number_of // 2 * 2:2]
    slack = jnp.minimum(tallies[giver] - 1, reach - tallies[taker]) // 2
    slack = jnp.where((giver == ranking[0]) | (taker == ranking[0]) | (tallies[taker] == 0), 0, jnp.maximum(slack, 0))
    moved = jax.random.randint(jax.random.fold_in(own, 4), (number_of // 2,), 0, 1 << 20) % (slack + 1)
    tallies = tallies.at[giver].add(-moved).at[taker].add(moved)
    items = jnp.searchsorted(jnp.cumsum(tallies), jnp.arange(rows * top), side="right").astype(jnp.int32)
    listing = items.reshape(top, rows).T
    listing = listing[jax.random.permutation(jax.random.fold_in(own, 1), rows)]
    turn = jax.random.randint(jax.random.fold_in(own, 2), (rows, 1), 0, top)
    return jnp.take_along_axis(listing, (jnp.arange(top)[None, :] + turn) % top, axis=1)


def load_shares(number_of, total, limit, skew, full):
    loads = [(1 << 20) // math.isqrt(standing ** skew) + 1 for standing in range(1, number_of + 1)]
    largest = limit if full else min(limit, max(-(-total // number_of), total * loads[0] // sum(loads)))
    least = 1 if total - largest >= number_of - 1 else 0
    counts, spare = [largest] + [least] * (number_of - 1), total - largest - least * (number_of - 1)
    while spare > 0:
        movable = [i for i in range(1, number_of) if counts[i] < largest] or [i for i in range(1, number_of) if counts[i] < limit]
        mass, remaining = sum([loads[i] for i in movable]), spare
        for i in movable:
            more = min(limit - counts[i], max(1, remaining * loads[i] // mass), spare)
            counts[i] = counts[i] + more
            spare = spare - more
    return np.array(counts)


def gaussian(own_key, dims, deviation, limit, pieces=(), held_as=jnp.bfloat16):
    drawn = jax.random.normal(own_key, dims, jnp.float32) * deviation
    if len(pieces) > 0:
        drawn = level_of(own_key, dims, pieces, -0.22, 0.18) * drawn
    return jnp.clip(drawn, min=-limit, max=limit).astype(held_as)


def setup_inputs(seed: int = 0) -> dict:
    key_of = jax.random.split(jax.random.key(seed), 8)
    tokens = gaussian(key_of[0], (TOKENS, D), 1.0, 6.0, ((0, 32),))
    routes_keys = jax.random.split(jax.random.fold_in(key_of[1], 1), TOKENS // TOK_DEV)
    routes_turns = jax.random.permutation(jax.random.fold_in(key_of[1], 3), TOKENS // TOK_DEV)
    routes = jax.vmap(lambda own, number: routed_block(jax.random.fold_in(key_of[1], 2), own, number, TOK_DEV, EXPERTS, TOP, CAP, 2))(routes_keys, routes_turns).reshape((TOKENS, TOP))
    route_gates = jnp.clip(jnp.exp(math.log(1.0) - 2.3025851 * jax.random.uniform(key_of[2], (TOKENS, TOP), jnp.float32) ** level_of(key_of[2], (TOKENS, TOP), ((0, 32),), -0.2, 0.2)), 0.1, 1.0)
    w_gate = gaussian(key_of[3], (EXPERTS, D, FF), D ** -0.5, 0.125, ((0, 4),))
    w_up = gaussian(key_of[4], (EXPERTS, D, FF), D ** -0.5, 0.125, ((0, 4),))
    w_down = gaussian(key_of[5], (EXPERTS, FF, D), FF ** -0.5, 0.3125, ((0, 4),))
    cotangent = gaussian(key_of[6], (TOKENS, D), 1.0, 6.0, ((0, 32),))
    return {"tokens": tokens, "routes": routes, "route_gates": route_gates, "w_gate": w_gate, "w_up": w_up, "w_down": w_down, "cotangent": cotangent}


def reference(tokens, routes, route_gates, w_gate, w_up, w_down, cotangent):
    flattened = routes.reshape(-1)
    gate_flat = route_gates.reshape(-1)
    bound_rows = N_DP * N_EXPERT * CAP
    grad_scale = 1.0 / ((TOP * TOK_DEV * N_DP) ** 0.5)

    def per_expert(state_tuple, expert_id):
        mixed_acc, tokens_acc, gates_acc = state_tuple
        is_routed = flattened == expert_id
        row_index = jnp.nonzero(is_routed, size=bound_rows, fill_value=0)[0].astype(jnp.int32)
        is_live = jnp.arange(bound_rows, dtype=jnp.int32) < jnp.sum(is_routed.astype(jnp.int32))
        token_row = (row_index // TOP).astype(jnp.int32)
        expert_input = jnp.where(is_live[:, None], tokens[token_row], jnp.zeros((), tokens.dtype))
        gate_value = jnp.where(is_live, gate_flat[row_index], jnp.zeros((), gate_flat.dtype))
        gate_matrix = w_gate[expert_id]
        up_matrix = w_up[expert_id]
        down_matrix = w_down[expert_id]
        pre_gate = jnp.dot(expert_input, gate_matrix, preferred_element_type=jnp.float32)
        pre_up = jnp.dot(expert_input, up_matrix, preferred_element_type=jnp.float32)
        sigmoid_gate = jax.nn.sigmoid(pre_gate)
        hidden = (pre_gate * sigmoid_gate * pre_up).astype(jnp.bfloat16)
        expert_out = jnp.dot(hidden, down_matrix, preferred_element_type=jnp.float32).astype(jnp.bfloat16)
        out_wide = expert_out.astype(jnp.float32)
        mixed_acc = mixed_acc.at[token_row].add(gate_value[:, None] * out_wide)
        grad_rows = cotangent[token_row].astype(jnp.float32)
        inner_sum = jnp.sum(grad_rows * out_wide, axis=1)
        gates_acc = gates_acc.at[row_index].add(jnp.where(is_live, inner_sum, jnp.zeros((), inner_sum.dtype)))
        grad_out = (gate_value[:, None] * grad_rows).astype(jnp.bfloat16)
        grad_hidden = jnp.dot(grad_out, down_matrix.T, preferred_element_type=jnp.float32)
        grad_gate = (grad_hidden * pre_up * sigmoid_gate * (1.0 + pre_gate * (1.0 - sigmoid_gate))).astype(jnp.bfloat16)
        grad_up = (grad_hidden * pre_gate * sigmoid_gate).astype(jnp.bfloat16)
        grad_input = (jnp.dot(grad_gate, gate_matrix.T, preferred_element_type=jnp.float32)
                      + jnp.dot(grad_up, up_matrix.T, preferred_element_type=jnp.float32)).astype(jnp.bfloat16)
        tokens_acc = tokens_acc.at[token_row].add(grad_input.astype(jnp.float32))
        down_grad = (jnp.dot(hidden.T, grad_out, preferred_element_type=jnp.float32) * grad_scale).astype(jnp.bfloat16)
        return (mixed_acc, tokens_acc, gates_acc), down_grad

    start_state = (jnp.zeros((TOKENS, D), jnp.float32), jnp.zeros((TOKENS, D), jnp.float32),
                   jnp.zeros((TOKENS * TOP,), jnp.float32))
    final_state, down_all = lax.scan(per_expert, start_state, jnp.arange(EXPERTS, dtype=jnp.int32))
    mixed_acc, tokens_acc, gates_acc = final_state
    return (mixed_acc.astype(jnp.bfloat16), tokens_acc.astype(jnp.bfloat16),
            gates_acc.reshape(TOKENS, TOP), down_all)
```

```python
import functools
import math

import jax
import jax.numpy as jnp
from jax import lax
from jax.experimental import pallas as pl
from jax.experimental.pallas import tpu as pltpu
from jax.sharding import PartitionSpec as P

MESH = pl.DeviceIdType.MESH
F32 = jnp.float32
BF16 = jnp.bfloat16
ROWS = (((1,), (0,)), ((), ()))
BOTH_LAST = (((1,), (1,)), ((), ()))
BOTH_FIRST = (((0,), (0,)), ((), ()))
X, G, OUT, GI = range(4)


def dot(a, b, dims=ROWS):
    return lax.dot_general(a, b, dims, preferred_element_type=F32)


def joined(ref, count):
    return jnp.concatenate([ref[e].astype(F32) for e in range(count)], axis=0).astype(BF16)


def kernel(
    n, n_dp, cap, scale,
    tokens, routes, gates, w_gate_hbm, w_up_hbm, w_down_hbm, cotangent,
    mixed, d_tokens, d_gates, d_w_down,
    x_send, g_send, out_send, gi_send, x_recv, g_recv, out_recv, gi_recv,
    part_send, part_recv, w_gate, w_up, w_down, weighted,
    send_sem, recv_sem, part_send_sem, part_recv_sem, weight_sem,
):
    me = lax.axis_index("expert")
    my_dp = lax.axis_index("dp")
    t = tokens.shape[0]

    weight_copies = [
        pltpu.make_async_copy(src.at[0], dst, weight_sem.at[i])
        for i, (src, dst) in enumerate(
            ((w_gate_hbm, w_gate), (w_up_hbm, w_up), (w_down_hbm, w_down))
        )
    ]
    for copy in weight_copies:
        copy.start()

    barrier = pltpu.get_barrier_semaphore()
    for k in range(1, n):
        pl.semaphore_signal(
            barrier, inc=1, device_id={"expert": lax.rem(me + k, n)}, device_id_type=MESH
        )
    for k in range(1, n_dp):
        pl.semaphore_signal(
            barrier, inc=1, device_id={"dp": lax.rem(my_dp + k, n_dp)}, device_id_type=MESH
        )

    row = routes[...].astype(F32)
    first = lax.broadcasted_iota(jnp.int32, (t, t), 0)
    second = lax.broadcasted_iota(jnp.int32, (t, t), 1)
    eye = first == second
    column = jnp.sum(jnp.where(eye, row, 0.0), axis=1, keepdims=True)
    same = column == row
    target_row = row * cap + jnp.sum(
        jnp.where(same & (first < second), 1.0, 0.0), axis=0, keepdims=True
    )
    target_column = column * cap + jnp.sum(
        jnp.where(same & (second < first), 1.0, 0.0), axis=1, keepdims=True
    )
    gate_column = jnp.sum(jnp.where(eye, gates[...], 0.0), axis=1, keepdims=True)
    slot = lax.broadcasted_iota(jnp.int32, (cap, t), 0)

    def pick(expert):
        return jnp.where((slot + expert * cap).astype(F32) == target_row, 1.0, 0.0).astype(BF16)

    def exchange(kind, k, source, landing):
        return pltpu.make_async_remote_copy(
            src_ref=source,
            dst_ref=landing.at[me],
            send_sem=send_sem.at[kind, k],
            recv_sem=recv_sem.at[kind, k],
            device_id={"expert": lax.rem(me + k, n)},
            device_id_type=MESH,
        )

    picks = [pick(lax.rem(me + k, n)) for k in range(n)]
    sends = [[], [], [], []]
    for k in range(1, n):
        x_send[k] = dot(picks[k], tokens[...]).astype(BF16)
        if k == 1:
            pl.semaphore_wait(barrier, n + n_dp - 2)
        sends[X].append(exchange(X, k, x_send.at[k], x_recv))
        sends[X][-1].start()
    weighted[...] = (gate_column * cotangent[...].astype(F32)).astype(BF16)
    for k in range(1, n):
        g_send[k] = dot(picks[k], weighted[...]).astype(BF16)
        sends[G].append(exchange(G, k, g_send.at[k], g_recv))
        sends[G][-1].start()
    x_recv[me] = dot(picks[0], tokens[...]).astype(BF16)
    g_recv[me] = dot(picks[0], weighted[...]).astype(BF16)

    for copy in weight_copies:
        copy.wait()
    for copy in sends[X]:
        copy.wait_recv()
    x = joined(x_recv, n)
    pre_gate = dot(x, w_gate[...])
    pre_up = dot(x, w_up[...])
    sigmoid = jax.nn.sigmoid(pre_gate)
    hidden = (pre_gate * sigmoid * pre_up).astype(BF16)
    out = dot(hidden, w_down[...])
    for e in range(n):
        out_send[e] = out[e * cap : (e + 1) * cap].astype(BF16)
    for k in range(1, n):
        sends[OUT].append(exchange(OUT, k, out_send.at[lax.rem(me + k, n)], out_recv))
        sends[OUT][-1].start()
    out_recv[me] = out_send[me]

    for copy in sends[G]:
        copy.wait_recv()
    g = joined(g_recv, n)
    grad_hidden = dot(g, w_down[...], BOTH_LAST)
    grad_gate = (grad_hidden * pre_up * sigmoid * (1.0 + pre_gate * (1.0 - sigmoid))).astype(BF16)
    grad_up = (grad_hidden * pre_gate * sigmoid).astype(BF16)
    grad_in = dot(grad_gate, w_gate[...], BOTH_LAST) + dot(grad_up, w_up[...], BOTH_LAST)
    for e in range(n):
        gi_send[e] = grad_in[e * cap : (e + 1) * cap].astype(BF16)
    for k in range(1, n):
        sends[GI].append(exchange(GI, k, gi_send.at[lax.rem(me + k, n)], gi_recv))
        sends[GI][-1].start()
    gi_recv[me] = gi_send[me]

    product = dot(hidden, g, BOTH_FIRST) * scale
    part_rows = product.shape[0] // n_dp
    for j in range(n_dp):
        part_send[j] = product[j * part_rows : (j + 1) * part_rows].astype(BF16)
    parts = []
    for k in range(1, n_dp):
        peer = lax.rem(my_dp + k, n_dp)
        parts.append(
            pltpu.make_async_remote_copy(
                src_ref=part_send.at[peer],
                dst_ref=part_recv.at[k],
                send_sem=part_send_sem.at[k],
                recv_sem=part_recv_sem.at[k],
                device_id={"dp": peer},
                device_id_type=MESH,
            )
        )
        parts[-1].start()

    spread = jnp.where(
        lax.broadcasted_iota(jnp.int32, (t, n * cap), 1).astype(F32) == target_column, 1.0, 0.0
    ).astype(BF16)
    for copy in sends[OUT]:
        copy.wait_recv()
    rows = dot(spread, joined(out_recv, n))
    mixed[...] = (gate_column * rows).astype(BF16)
    inner = jnp.sum(cotangent[...].astype(F32) * rows, axis=1, keepdims=True)
    d_gates[...] = jnp.sum(jnp.where(eye, inner, 0.0), axis=0, keepdims=True)

    total = part_send[my_dp].astype(F32)
    for k, copy in enumerate(parts, 1):
        copy.wait_recv()
        total = total + part_recv[k].astype(F32)
    d_w_down[0] = total.astype(BF16)

    for copy in sends[GI]:
        copy.wait_recv()
    d_tokens[...] = dot(spread, joined(gi_recv, n)).astype(BF16)
    for copies in (*sends, parts):
        for copy in copies:
            copy.wait_send()


def per_device(n, n_dp, tokens, routes, route_gates, w_gate, w_up, w_down, cotangent):
    t, d = tokens.shape
    ff = w_down.shape[1]
    cap = 5 * t // (4 * n)
    cap = -(-cap // 8) * 8
    scale = 1.0 / math.sqrt(routes.shape[1] * t * n_dp)
    vmem = pl.BlockSpec(memory_space=pltpu.VMEM)
    hbm = pl.BlockSpec(memory_space=pl.ANY)
    block = pltpu.VMEM((n, cap, d), BF16)
    part = pltpu.VMEM((n_dp, ff // n_dp, d), BF16)
    mixed, d_tokens, d_gates, d_w_down = pl.pallas_call(
        functools.partial(kernel, n, n_dp, cap, scale),
        out_shape=(
            jax.ShapeDtypeStruct((t, d), BF16),
            jax.ShapeDtypeStruct((t, d), BF16),
            jax.ShapeDtypeStruct((1, t), F32),
            jax.ShapeDtypeStruct((1, ff // n_dp, d), BF16),
        ),
        in_specs=[vmem, vmem, vmem, hbm, hbm, hbm, vmem],
        out_specs=(vmem,) * 4,
        scratch_shapes=[block] * 8
        + [part] * 2
        + [
            pltpu.VMEM((d, ff), BF16),
            pltpu.VMEM((d, ff), BF16),
            pltpu.VMEM((ff, d), BF16),
            pltpu.VMEM((t, d), BF16),
            pltpu.SemaphoreType.DMA((4, n)),
            pltpu.SemaphoreType.DMA((4, n)),
            pltpu.SemaphoreType.DMA((n_dp,)),
            pltpu.SemaphoreType.DMA((n_dp,)),
            pltpu.SemaphoreType.DMA((3,)),
        ],
        compiler_params=pltpu.CompilerParams(
            collective_id=0, has_side_effects=True, vmem_limit_bytes=56 * 2**20
        ),
    )(
        tokens, routes.reshape(1, t), route_gates.reshape(1, t),
        w_gate, w_up, w_down, cotangent,
    )
    return mixed, d_tokens, d_gates.reshape(t, 1), d_w_down


def solution(mesh):
    split = P(("dp", "expert"), None)
    weights = P("expert", None, None)
    return jax.shard_map(
        functools.partial(per_device, mesh.shape["expert"], mesh.shape["dp"]),
        mesh=mesh,
        in_specs=(split, split, split, weights, weights, weights, split),
        out_specs=(split, split, split, P("expert", "dp", None)),
        check_vma=False,
    )
```

```python
import functools
import math

import jax
import jax.numpy as jnp
from jax import lax
from jax.experimental import pallas as pl
from jax.experimental.pallas import tpu as pltpu
from jax.sharding import PartitionSpec as P

MESH = pl.DeviceIdType.MESH
F32 = jnp.float32
BF16 = jnp.bfloat16
ROWS = (((1,), (0,)), ((), ()))
BOTH_LAST = (((1,), (1,)), ((), ()))
BOTH_FIRST = (((0,), (0,)), ((), ()))
X, G, OUT, GI = range(4)


def dot(a, b, dims=ROWS):
    return lax.dot_general(a, b, dims, preferred_element_type=F32)


def joined(ref, count):
    return jnp.concatenate([ref[e].astype(F32) for e in range(count)], axis=0).astype(BF16)


def kernel(
    n, n_dp, cap, scale,
    tokens_hbm, routes, gates, w_gate_hbm, w_up_hbm, w_down_hbm, cotangent_hbm,
    mixed_hbm, d_tokens_hbm, d_gates_hbm, d_w_down_hbm,
    tokens, cotangent, mixed, d_tokens, d_gates, d_w_down,
    x_send, g_send, out_send, gi_send, x_recv, g_recv, out_recv, gi_recv,
    part_send, part_recv, w_gate, w_up, w_down, weighted,
    send_sem, recv_sem, part_send_sem, part_recv_sem, weight_sem, row_sem, result_sem,
):
    me = lax.axis_index("expert")
    my_dp = lax.axis_index("dp")
    t = tokens.shape[0]

    barrier = pltpu.get_barrier_semaphore()
    for k in range(1, n):
        pl.semaphore_signal(
            barrier, inc=1, device_id={"expert": lax.rem(me + k, n)}, device_id_type=MESH
        )
    for k in range(1, n_dp):
        pl.semaphore_signal(
            barrier, inc=1, device_id={"dp": lax.rem(my_dp + k, n_dp)}, device_id_type=MESH
        )

    row_copies = [
        pltpu.make_async_copy(src, dst, row_sem.at[i])
        for i, (src, dst) in enumerate(((tokens_hbm, tokens), (cotangent_hbm, cotangent)))
    ]
    for copy in row_copies:
        copy.start()
    results = [
        pltpu.make_async_copy(src, dst, result_sem.at[i])
        for i, (src, dst) in enumerate(
            (
                (mixed, mixed_hbm),
                (d_tokens, d_tokens_hbm),
                (d_gates, d_gates_hbm),
                (d_w_down, d_w_down_hbm),
            )
        )
    ]
    weight_copies = [
        pltpu.make_async_copy(src.at[0], dst, weight_sem.at[i])
        for i, (src, dst) in enumerate(
            ((w_gate_hbm, w_gate), (w_up_hbm, w_up), (w_down_hbm, w_down))
        )
    ]
    for copy in weight_copies:
        copy.start()

    row = routes[...].astype(F32)
    first = lax.broadcasted_iota(jnp.int32, (t, t), 0)
    second = lax.broadcasted_iota(jnp.int32, (t, t), 1)
    eye = first == second
    column = jnp.sum(jnp.where(eye, row, 0.0), axis=1, keepdims=True)
    same = column == row
    target_row = row * cap + jnp.sum(
        jnp.where(same & (first < second), 1.0, 0.0), axis=0, keepdims=True
    )
    target_column = column * cap + jnp.sum(
        jnp.where(same & (second < first), 1.0, 0.0), axis=1, keepdims=True
    )
    gate_column = jnp.sum(jnp.where(eye, gates[...], 0.0), axis=1, keepdims=True)
    slot = lax.broadcasted_iota(jnp.int32, (cap, t), 0)

    def pick(expert):
        return jnp.where((slot + expert * cap).astype(F32) == target_row, 1.0, 0.0).astype(BF16)

    def exchange(kind, k, source, landing):
        return pltpu.make_async_remote_copy(
            src_ref=source,
            dst_ref=landing.at[me],
            send_sem=send_sem.at[kind, k],
            recv_sem=recv_sem.at[kind, k],
            device_id={"expert": lax.rem(me + k, n)},
            device_id_type=MESH,
        )

    row_copies[0].wait()
    picks = [pick(lax.rem(me + k, n)) for k in range(n)]
    sends = [[], [], [], []]
    for k in range(1, n):
        x_send[k] = dot(picks[k], tokens[...]).astype(BF16)
        if k == 1:
            pl.semaphore_wait(barrier, n + n_dp - 2)
        sends[X].append(exchange(X, k, x_send.at[k], x_recv))
        sends[X][-1].start()
    row_copies[1].wait()
    weighted[...] = (gate_column * cotangent[...].astype(F32)).astype(BF16)
    for k in range(1, n):
        g_send[k] = dot(picks[k], weighted[...]).astype(BF16)
        sends[G].append(exchange(G, k, g_send.at[k], g_recv))
        sends[G][-1].start()
    x_recv[me] = dot(picks[0], tokens[...]).astype(BF16)
    g_recv[me] = dot(picks[0], weighted[...]).astype(BF16)

    for copy in weight_copies:
        copy.wait()
    for copy in sends[X]:
        copy.wait_recv()
    x = joined(x_recv, n)
    pre_gate = dot(x, w_gate[...])
    pre_up = dot(x, w_up[...])
    sigmoid = jax.nn.sigmoid(pre_gate)
    hidden = (pre_gate * sigmoid * pre_up).astype(BF16)
    out = dot(hidden, w_down[...])
    for e in range(n):
        out_send[e] = out[e * cap : (e + 1) * cap].astype(BF16)
    for k in range(1, n):
        sends[OUT].append(exchange(OUT, k, out_send.at[lax.rem(me + k, n)], out_recv))
        sends[OUT][-1].start()
    out_recv[me] = out_send[me]

    for copy in sends[G]:
        copy.wait_recv()
    g = joined(g_recv, n)
    grad_hidden = dot(g, w_down[...], BOTH_LAST)
    grad_gate = (grad_hidden * pre_up * sigmoid * (1.0 + pre_gate * (1.0 - sigmoid))).astype(BF16)
    grad_up = (grad_hidden * pre_gate * sigmoid).astype(BF16)
    grad_in = dot(grad_gate, w_gate[...], BOTH_LAST) + dot(grad_up, w_up[...], BOTH_LAST)
    for e in range(n):
        gi_send[e] = grad_in[e * cap : (e + 1) * cap].astype(BF16)
    for k in range(1, n):
        sends[GI].append(exchange(GI, k, gi_send.at[lax.rem(me + k, n)], gi_recv))
        sends[GI][-1].start()
    gi_recv[me] = gi_send[me]

    product = dot(hidden, g, BOTH_FIRST) * scale
    part_rows = product.shape[0] // n_dp
    for j in range(n_dp):
        part_send[j] = product[j * part_rows : (j + 1) * part_rows].astype(BF16)
    parts = []
    for k in range(1, n_dp):
        peer = lax.rem(my_dp + k, n_dp)
        parts.append(
            pltpu.make_async_remote_copy(
                src_ref=part_send.at[peer],
                dst_ref=part_recv.at[k],
                send_sem=part_send_sem.at[k],
                recv_sem=part_recv_sem.at[k],
                device_id={"dp": peer},
                device_id_type=MESH,
            )
        )
        parts[-1].start()

    spread = jnp.where(
        lax.broadcasted_iota(jnp.int32, (t, n * cap), 1).astype(F32) == target_column, 1.0, 0.0
    ).astype(BF16)
    for copy in sends[OUT]:
        copy.wait_recv()
    rows = dot(spread, joined(out_recv, n))
    mixed[...] = (gate_column * rows).astype(BF16)
    inner = jnp.sum(cotangent[...].astype(F32) * rows, axis=1, keepdims=True)
    d_gates[...] = jnp.sum(jnp.where(eye, inner, 0.0), axis=0, keepdims=True)
    results[0].start()
    results[2].start()

    total = part_send[my_dp].astype(F32)
    for k, copy in enumerate(parts, 1):
        copy.wait_recv()
        total = total + part_recv[k].astype(F32)
    d_w_down[0] = total.astype(BF16)
    results[3].start()

    for copy in sends[GI]:
        copy.wait_recv()
    d_tokens[...] = dot(spread, joined(gi_recv, n)).astype(BF16)
    results[1].start()
    for copies in (*sends, parts):
        for copy in copies:
            copy.wait_send()
    for copy in results:
        copy.wait()


def hand_over(count, *refs):
    made, results, held = refs[:count], refs[count : 2 * count], refs[2 * count : 3 * count]
    read_sem, write_sem = refs[3 * count :]
    reads = [pltpu.make_async_copy(made[i], held[i], read_sem.at[i]) for i in range(count)]
    writes = [pltpu.make_async_copy(held[i], results[i], write_sem.at[i]) for i in range(count)]
    for copy in reads:
        copy.start()
    for read, write in zip(reads, writes):
        read.wait()
        write.start()
    for copy in writes:
        copy.wait()


def per_device(n, n_dp, tokens, routes, route_gates, w_gate, w_up, w_down, cotangent):
    t, d = tokens.shape
    ff = w_down.shape[1]
    cap = 5 * t // (4 * n)
    cap = -(-cap // 8) * 8
    scale = 1.0 / math.sqrt(routes.shape[1] * t * n_dp)
    vmem = pl.BlockSpec(memory_space=pltpu.VMEM)
    hbm = pl.BlockSpec(memory_space=pl.ANY)
    block = pltpu.VMEM((n, cap, d), BF16)
    part = pltpu.VMEM((n_dp, ff // n_dp, d), BF16)
    shapes = (
        jax.ShapeDtypeStruct((t, d), BF16),
        jax.ShapeDtypeStruct((t, d), BF16),
        jax.ShapeDtypeStruct((1, t), F32),
        jax.ShapeDtypeStruct((1, ff // n_dp, d), BF16),
    )
    made = pl.pallas_call(
        functools.partial(kernel, n, n_dp, cap, scale),
        out_shape=shapes,
        in_specs=[hbm, vmem, vmem, hbm, hbm, hbm, hbm],
        out_specs=(hbm,) * 4,
        scratch_shapes=[
            pltpu.VMEM(s.shape, s.dtype) for s in (shapes[0], shapes[0], *shapes)
        ]
        + [block] * 8
        + [part] * 2
        + [
            pltpu.VMEM((d, ff), BF16),
            pltpu.VMEM((d, ff), BF16),
            pltpu.VMEM((ff, d), BF16),
            pltpu.VMEM((t, d), BF16),
            pltpu.SemaphoreType.DMA((4, n)),
            pltpu.SemaphoreType.DMA((4, n)),
            pltpu.SemaphoreType.DMA((n_dp,)),
            pltpu.SemaphoreType.DMA((n_dp,)),
            pltpu.SemaphoreType.DMA((3,)),
            pltpu.SemaphoreType.DMA((2,)),
            pltpu.SemaphoreType.DMA((4,)),
        ],
        compiler_params=pltpu.CompilerParams(
            collective_id=0, has_side_effects=True, vmem_limit_bytes=56 * 2**20
        ),
    )(
        tokens, routes.reshape(1, t), route_gates.reshape(1, t),
        w_gate, w_up, w_down, cotangent,
    )
    mixed, d_tokens, d_gates, d_w_down = pl.pallas_call(
        functools.partial(hand_over, len(shapes)),
        out_shape=shapes,
        in_specs=[hbm] * 4,
        out_specs=(hbm,) * 4,
        scratch_shapes=[pltpu.VMEM(s.shape, s.dtype) for s in shapes]
        + [pltpu.SemaphoreType.DMA((len(shapes),))] * 2,
    )(*made)
    return mixed, d_tokens, d_gates.reshape(t, 1), d_w_down


def solution(mesh):
    split = P(("dp", "expert"), None)
    weights = P("expert", None, None)
    return jax.shard_map(
        functools.partial(per_device, mesh.shape["expert"], mesh.shape["dp"]),
        mesh=mesh,
        in_specs=(split, split, split, weights, weights, weights, split),
        out_specs=(split, split, split, P("expert", "dp", None)),
        check_vma=False,
    )
```
